512 devices in a mesh: ctx: 32 (over x, z), head: 16 (over y, core).
Axes of the slice: x: 4, y: 8, z: 8, core: 2. Of those that a mesh axis runs over, the one named last changes fastest.
Arguments:
- queries: bfloat16 [4096, 4096], P('ctx', 'head'), may hold values from -24 to 24
- key_rows: bfloat16 [4096, 4096], P('ctx', 'head'), may hold values from -24 to 24
- value_rows: bfloat16 [4096, 4096], P('ctx', 'head'), may hold values from -6 to 6
- upstream: bfloat16 [4096, 6144], P('ctx', 'head'), may hold values from -6 to 6
- out_weight: bfloat16 [6144, 4096], P('ctx', 'head'), may hold values from -0.078125 to 0.078125
- group_ids: int32 [4096], replicated, may hold values from 0 to 31, never falling along the last dimension, each value on 1 to 256 neighbouring positions
Outputs:
- grad_queries: bfloat16 [4096, 4096], P('ctx', 'head')
- grad_keys: bfloat16 [4096, 4096], P('ctx', 'head')
- grad_values: bfloat16 [4096, 4096], P('ctx', 'head')
The draws below stay inside these ranges and needn't reach their ends.
Inputs may be any that keep to these rules, and one draw needn't show every extreme that they name: `group_ids`: never falling along the tokens; each group number covers 1 to 256 consecutive tokens, one exactly 256.
All inputs are finite; a program needn't handle non-finite values.
Results may differ from the reference program's by a relative error of at most 0.025.
Values may be sent and summed in bfloat16 or wider, within the bound.
A program may use at most 64 MiB of HBM per device.

```python
import math
import jax
import jax.numpy as jnp
import numpy as np
from jax import lax

D = 6144
HEADS = 32
HDIM = 128
GROUP = 128
TOKENS = 4096


def drawn_pair(key):
    full_width = HEADS * HDIM
    query_base = jnp.clip(jax.random.normal(jax.random.fold_in(key, 101), (TOKENS, full_width), jnp.float32), -6.0, 6.0)
    key_base = jnp.clip(jax.random.normal(jax.random.fold_in(key, 102), (TOKENS, full_width), jnp.float32), -6.0, 6.0)
    return (query_base, key_base)


def draw_queries(key, part):
    return drawn_pair(key)[0].astype(jnp.bfloat16)


def draw_key_rows(key, part):
    return drawn_pair(key)[1].astype(jnp.bfloat16)


def block_levels(own_key, dims, shards, low, high):
    def one(dim, shards_of):
        heights = jax.random.uniform(jax.random.fold_in(jax.random.fold_in(own_key, 6), dim), (shards_of,), jnp.float32, low / len(shards), high / len(shards))
        return jnp.repeat(jnp.exp(heights), dims[dim] // shards_of).reshape((-1,) + (1,) * (len(dims) - dim - 1))

    factor_of = one(*shards[0])
    for cut in shards[1:]:
        factor_of = factor_of * one(*cut)
    return factor_of


def length_profile(count, total, limit, slope):
    portions = [(1 << 20) // math.isqrt(standing ** slope) + 1 for standing in range(2, count + 1)]
    surplus, given = total - limit - (count - 1), [1] * (count - 1)
    while surplus > 0:
        movable = [i for i in range(count - 1) if given[i] < limit]
        whole, left = sum([portions[i] for i in movable]), surplus
        for i in movable:
            more = min(limit - given[i], max(1, left * portions[i] // whole), surplus)
            given[i] = given[i] + more
            surplus = surplus - more
    return np.array([limit] + given)


def ragged(stream_key, count, total, bound, slope):
    if count == 2:
        one = jax.random.randint(stream_key, (), max(1, total - bound), min(bound, total - 1) + 1)
        return jnp.stack([one, total - one])
    tallies = jnp.asarray(length_profile(count, total, bound, slope), jnp.int32)
    pairs = (count - 1) // 2
    giver, taker = tallies[1:1 + 2 * pairs:2], tallies[2:2 + 2 * pairs:2]
    room = jnp.minimum(giver - 1, bound - taker)
    passed = jax.random.randint(jax.random.fold_in(stream_key, 1), (pairs,), 0, 1 << 20) % (room + 1)
    tallies = tallies.at[1:1 + 2 * pairs:2].set(giver - passed).at[2:2 + 2 * pairs:2].set(taker + passed)
    return tallies[jax.random.permutation(jax.random.fold_in(stream_key, 2), count)]


def scatter_about(rng, extent, scale, most, split=(), kind=jnp.bfloat16):
    drawn = scale * jax.random.normal(rng, extent, jnp.float32)
    if split:
        drawn = drawn * block_levels(rng, extent, split, -0.22, 0.18)
    return jnp.clip(drawn, -most, most).astype(kind)


def setup_inputs(seed: int = 0) -> dict:
    key_of = jax.random.split(jax.random.key(seed), 7)
    queries = draw_queries(jax.random.fold_in(key_of[6], 71), 0)
    key_rows = draw_key_rows(jax.random.fold_in(key_of[6], 71), 0)
    value_rows = scatter_about(key_of[2], (TOKENS, HEADS * HDIM), 1.0, 6.0, ((0, 32), (1, 16)))
    upstream = scatter_about(key_of[3], (TOKENS, D), 1.0, 6.0, ((0, 32), (1, 16)))
    out_weight = scatter_about(key_of[4], (D, HEADS * HDIM), D ** -0.5, 0.078125, ((0, 32), (1, 16)))
    group_ids = jnp.searchsorted(jnp.cumsum(ragged(key_of[5], TOKENS // GROUP, TOKENS, 2 * GROUP, 1)), jnp.arange(TOKENS), side="right").astype(jnp.int32)
    return dict(queries=queries, key_rows=key_rows, value_rows=value_rows, upstream=upstream, out_weight=out_weight, group_ids=group_ids)


def reference(queries, key_rows, value_rows, upstream, out_weight, group_ids):
    scaling = HDIM ** -0.5
    grad_out = jnp.dot(upstream, out_weight, preferred_element_type=jnp.float32).astype(jnp.bfloat16)
    total_rows = queries.shape[0]
    heads_all = queries.shape[1] // HDIM
    allowed = group_ids[None, :] <= group_ids[:, None]

    def heads_first(matrix):
        return matrix.reshape(total_rows, heads_all, HDIM).transpose(1, 0, 2)

    def one_head(operands):
        query_head, key_head, value_head, grad_head = operands
        scores = scaling * jnp.dot(query_head, key_head.T, preferred_element_type=jnp.float32)
        row_max = jnp.max(jnp.where(allowed, scores, -1.0e30), axis=1)
        weights = jnp.where(allowed, jnp.exp(scores - row_max[:, None]), 0.0)
        log_total = row_max + jnp.log(jnp.sum(weights, axis=1))
        probs = jnp.where(allowed, jnp.exp(scores - log_total[:, None]), 0.0)
        probs_low = probs.astype(jnp.bfloat16)
        attn_out = jnp.dot(probs_low, value_head, preferred_element_type=jnp.float32)
        delta = jnp.sum(grad_head.astype(jnp.float32) * attn_out, axis=1)
        grad_probs = jnp.dot(grad_head, value_head.T, preferred_element_type=jnp.float32)
        mixed = (probs * grad_probs).astype(jnp.bfloat16)
        grad_query = scaling * (jnp.dot(mixed, key_head, preferred_element_type=jnp.float32)
                                - delta[:, None] * jnp.dot(probs_low, key_head, preferred_element_type=jnp.float32))
        grad_scores = (probs * (grad_probs - delta[:, None])).astype(jnp.bfloat16)
        grad_key = scaling * jnp.dot(grad_scores.T, query_head, preferred_element_type=jnp.float32)
        grad_value = jnp.dot(probs_low.T, grad_head, preferred_element_type=jnp.float32)
        return (grad_query, grad_key, grad_value)

    results = lax.map(one_head, (heads_first(queries), heads_first(key_rows), heads_first(value_rows), heads_first(grad_out)))

    def tokens_first(stacked):
        return stacked.transpose(1, 0, 2).reshape(total_rows, heads_all * HDIM).astype(jnp.bfloat16)

    return (tokens_first(results[0]), tokens_first(results[1]), tokens_first(results[2]))
```

```python
import functools

import jax
import jax.numpy as jnp
from jax import lax
from jax.experimental import pallas as pl
from jax.experimental.pallas import tpu as pltpu
from jax.sharding import PartitionSpec as P

MESH = pl.DeviceIdType.MESH
HDIM = 128
LOG2E = 1.4426950408889634
MASKED = -1e30
FLOOR = -1e29
F32 = jnp.float32
BF16 = jnp.bfloat16


def kernel(
    X, Z, Y,
    gid, q, k, v, up, w,
    dq_out, dk_out, dv_out,
    ubuf, upx, wbuf, qbuf, kbuf, vbuf, acc, dsend, drecv, dobuf,
    ml_send, ml_recv, u_send, u_recv, kid, kt, p_s, dp_s, kpart, vpart,
    dqsend, dqrecv, dqacc, rsend, rrecv,
    us, ur, ws, wr, kvs, kvr, qs, qr, xs, xr, sbs, sbr,
    ds, dr_, os_, or_, ms, mr, es, er, gs, gr, rs, rr,
):
    K2 = Y // X
    WB = X * Z // (2 * Y)
    R = q.shape[0]
    Q = X * R
    i, j = lax.axis_index("ctx"), lax.axis_index("head")
    x, z = lax.div(i, Z), lax.rem(i, Z)
    y, c = lax.div(j, 2), lax.rem(j, 2)

    def dev(xx, zz, yy, cc):
        return (xx * Z + zz, yy * 2 + cc)

    def add(a, b, n):
        return lax.rem(a + b + n, n)

    def remote(src, dst, s_sem, r_sem, device):
        return pltpu.make_async_remote_copy(
            src_ref=src, dst_ref=dst, send_sem=s_sem, recv_sem=r_sem,
            device_id=device, device_id_type=MESH,
        )

    z_dev = (dev(x, add(z, 1, Z), y, c), dev(x, add(z, -1, Z), y, c))
    y_dev = (dev(x, z, add(y, 1, Y), c), dev(x, z, add(y, -1, Y), c))
    x_dev = [None] + [dev(add(x, d, X), z, y, c) for d in range(1, X)]
    x_src = [add(x, -d, X) for d in range(X)]
    sibling = dev(x, z, y, 1 - c)

    barrier = pltpu.get_barrier_semaphore()
    peers = [*z_dev, *y_dev, *x_dev[1:], sibling]
    for peer in peers:
        pl.semaphore_signal(barrier, inc=1, device_id=peer, device_id_type=MESH)
    pl.semaphore_wait(barrier, len(peers))

    pending = []

    class Ring:
        def __init__(self, n, me, devs, own, buf, s_sem, r_sem):
            self.n, self.me, self.devs = n, me, devs
            self.own, self.buf, self.s, self.r = own, buf, s_sem, r_sem
            self.last = n // 2 - 1

        def chunks(self, d, s):
            return (d,) if s == self.last else (d, 1 - d)

        def block(self, d, s):
            return add(self.me, -s if d == 0 else s, self.n)

        def send(self, d, s, h):
            b = self.block(d, s)
            src = self.own(h) if s == 0 else self.buf(b, h)
            copy = remote(
                src, self.buf(b, h), self.s.at[d, s, h], self.r.at[d, s, h], self.devs[d]
            )
            copy.start()
            pending.append(copy)

        def begin(self):
            for n in range(2):
                for d in range(2):
                    if n < len(self.chunks(d, 0)):
                        self.send(d, 0, self.chunks(d, 0)[n])

        def step(self, s):
            for n in range(2):
                for d in range(2):
                    if n < len(self.chunks(d, s)):
                        h = self.chunks(d, s)[n]
                        b = self.block(d, s + 1)
                        remote(
                            self.buf(b, h), self.buf(b, h), self.s.at[d, s, h],
                            self.r.at[d, s, h], self.devs[d],
                        ).wait_recv()
                        if s < self.last and h in self.chunks(d, s + 1):
                            self.send(d, s + 1, h)

    uh, wh = up.shape[0] // 2, w.shape[0] // 2
    ring_u = Ring(
        Y, y, y_dev,
        lambda h: up.at[pl.ds(h * uh, uh)],
        lambda b, h: ubuf.at[b, pl.ds(h * uh, uh)],
        us, ur,
    )
    ring_w = Ring(
        Z, z, z_dev,
        lambda h: w.at[pl.ds(h * wh, wh)],
        lambda b, h: wbuf.at[b, pl.ds(h * wh, wh)],
        ws, wr,
    )
    ring_kv = Ring(
        Z, z, z_dev,
        lambda h: (k, v)[h],
        lambda b, h: (kbuf, vbuf)[h].at[b],
        kvs, kvr,
    )

    relayed = []

    def relay(block, src, n):
        xt, kk = lax.div(block, K2), lax.rem(block, K2)
        d = add(xt, -x, X)

        def copy():
            return remote(
                src, upx.at[kk, c, x], xs.at[n], xr.at[d, kk], dev(xt, z, y, c)
            )

        @pl.when(d != 0)
        def _():
            copy().start()

        @pl.when(d == 0)
        def _():
            pltpu.make_async_copy(src, upx.at[kk, c, x], xr.at[d, kk]).start()

        relayed.append((d, copy))

    def exchange(src, dst, s_sem, r_sem):
        for d in range(1, X):
            copy = remote(src(add(x, d, X)), dst.at[x], s_sem.at[d], r_sem.at[d], x_dev[d])
            copy.start()
            pending.append(copy)

    def arrive(dst, s_sem, r_sem, d):
        ref = dst.at[x_src[d]]
        remote(ref, ref, s_sem.at[d], r_sem.at[d], x_dev[d]).wait_recv()

    ring_u.begin()
    ring_w.begin()
    relay(y, up, 0)
    exchange(lambda _: q, qbuf, qs, qr)
    wbuf[z] = w[...]
    kbuf[z] = k[...]
    vbuf[z] = v[...]
    qbuf[x] = q[...]
    kv_next = 0
    steps = max(Y, Z) // 2
    for s in range(steps):
        if s < Y // 2:
            ring_u.step(s)
            relay(ring_u.block(0, s + 1), ubuf.at[ring_u.block(0, s + 1)], 2 * s + 1)
            if s < Y // 2 - 1:
                relay(ring_u.block(1, s + 1), ubuf.at[ring_u.block(1, s + 1)], 2 * s + 2)
        if s < Z // 2:
            ring_w.step(s)
        if s == 0:
            ring_kv.begin()
        if s >= 2:
            ring_kv.step(kv_next)
            kv_next += 1

    for b in range(Z):
        row = gid[pl.ds(x * Z + b, 1), :].astype(F32)
        kid[b] = jnp.broadcast_to(row, (R, R)).T
    qid = jnp.concatenate([gid[pl.ds(b * Z + z, 1), :].astype(F32) for b in range(X)], axis=1)

    turn = lax.rem(y - K2 * x + Y * K2, Y)
    near = jnp.where((turn >= 1) & (turn <= Y // 2), 1, 0) if K2 > 1 else 0
    order = [near, 1 - near] if K2 == 2 else list(range(K2))

    def shared(n, kk):
        return remote(upx.at[kk, c], upx.at[kk, c], sbs.at[n], sbr.at[n], sibling)

    for n, kk in enumerate(order):
        for d in range(X):
            dst = upx.at[kk, c, x_src[d]]
            remote(dst, dst, xs.at[0], xr.at[d, kk], sibling).wait_recv()
        copy = shared(n, kk)
        copy.start()
        pending.append(copy)
    for n, kk in enumerate(order):
        shared(n, kk).wait_recv()
        total = None
        for cc in range(2):
            rows = upx[kk, cc].reshape(Q, upx.shape[4])
            weights = wbuf[pl.ds((kk * 2 + cc) * WB, WB)].reshape(upx.shape[4], w.shape[1])
            part = jnp.dot(rows, weights, preferred_element_type=F32)
            total = part if total is None else total + part
        total = total.reshape(acc.shape)
        if n > 0:
            total = total + acc[...]
        if n < K2 - 1:
            acc[...] = total
        else:
            acc[...] = total
            dsend[...] = total.astype(BF16)
    exchange(lambda t: dsend.at[t], drecv, ds, dr_)
    while kv_next < Z // 2 - 1:
        ring_kv.step(kv_next)
        kv_next += 1
    total = acc[x]
    for d in range(1, X):
        arrive(drecv, ds, dr_, d)
        total = total + drecv[x_src[d]].astype(F32)
    dobuf[x] = total.astype(BF16)
    exchange(lambda _: dobuf.at[x], dobuf, os_, or_)
    if kv_next < Z // 2:
        ring_kv.step(kv_next)
    for d in range(1, X):
        arrive(qbuf, qs, qr, d)

    NT = (((1,), (1,)), ((), ()))
    scale = HDIM ** (-0.5)
    cols = [slice(h * HDIM, (h + 1) * HDIM) for h in range(2)]

    def fold(block, op):
        return op(block.reshape(R // 8, 8, Q), axis=0)

    def loop_scores(b, maxima):
        allowed = jnp.tile(kid[b], (1, X)) <= qid
        out = []
        for h in range(2):
            queries = qbuf[:, :, cols[h]].reshape(Q, HDIM)
            s = lax.dot_general(kbuf[b, :, cols[h]], queries, NT, preferred_element_type=F32)
            s = jnp.where(allowed, s * (scale * LOG2E), MASKED)
            p_s[h, b] = s
            kt[b, cols[h], :] = kbuf[b, :, cols[h]].T
            out.append(jnp.maximum(maxima[h], fold(s, jnp.max)))
        return tuple(out)

    start = jnp.full((8, Q), FLOOR, F32)
    maxima = lax.fori_loop(0, Z, loop_scores, (start, start))
    m_own = [jnp.max(m, axis=0, keepdims=True) for m in maxima]

    def loop_exp(b, sums):
        out = []
        for h in range(2):
            e = jnp.exp2(p_s[h, b] - m_own[h])
            p_s[h, b] = e
            out.append(sums[h] + fold(e, jnp.sum))
        return tuple(out)

    zero = jnp.zeros((8, Q), F32)
    sums = lax.fori_loop(0, Z, loop_exp, (zero, zero))
    l_own = [jnp.sum(s, axis=0, keepdims=True) for s in sums]
    ml_send[...] = jnp.concatenate([*m_own, *l_own, jnp.zeros((4, Q), F32)], axis=0)
    exchange(lambda _: ml_send, ml_recv, ms, mr)
    stats = [ml_send[...]]
    for d in range(1, X):
        arrive(ml_recv, ms, mr, d)
        stats.append(ml_recv[x_src[d]])
    factor = []
    for h in range(2):
        m_all = functools.reduce(jnp.maximum, [s[h : h + 1] for s in stats])
        l_all = sum(s[2 + h : 3 + h] * jnp.exp2(s[h : h + 1] - m_all) for s in stats)
        factor.append(jnp.exp2(m_own[h] - m_all) / l_all)

    for d in range(1, X):
        arrive(dobuf, os_, or_, d)

    def loop_probs(b, sums):
        out = []
        for h in range(2):
            grads = dobuf[:, :, cols[h]].reshape(Q, HDIM)
            g = lax.dot_general(vbuf[b, :, cols[h]], grads, NT, preferred_element_type=F32)
            prob = p_s[h, b] * factor[h]
            p_s[h, b] = prob
            dp_s[h, b] = g
            vpart[b, h] = jnp.dot(prob.astype(BF16), grads, preferred_element_type=F32)
            out.append(sums[h] + fold(prob * g, jnp.sum))
        return tuple(out)

    sums = lax.fori_loop(0, Z, loop_probs, (zero, zero))
    u_own = [jnp.sum(s, axis=0, keepdims=True) for s in sums]
    u_send[...] = jnp.concatenate([*u_own, jnp.zeros((6, Q), F32)], axis=0)
    exchange(lambda _: u_send, u_recv, es, er)

    half = Z // 2
    parts = (vpart, kpart)
    factors = (1.0, scale)

    def rs_heads(d, t):
        return (d,) if t == 0 else (0, 1)

    def rs_copy(a, d, t):
        if t == 0:
            src, dst = rsend.at[a, d, t, d], rrecv.at[a, d, t, d]
        else:
            src, dst = rsend.at[a, d, t], rrecv.at[a, d, t]
        return remote(src, dst, rs.at[a, d, t], rr.at[a, d, t], z_dev[d])

    def rs_step(a, t):
        for d in range(2):
            target = add(z, (half - t) if d == 0 else (t - half), Z)
            if t > 0:
                rs_copy(a, d, t - 1).wait_recv()
            for h in rs_heads(d, t):
                value = parts[a][target, h] * factors[a]
                if t > 0 and h in rs_heads(d, t - 1):
                    value = value + rrecv[a, d, t - 1, h].astype(F32)
                rsend[a, d, t, h] = value.astype(BF16)
            copy = rs_copy(a, d, t)
            copy.start()
            pending.append(copy)

    def rs_end(a, out):
        for d in range(2):
            rs_copy(a, d, half - 1).wait_recv()
        for h in range(2):
            value = parts[a][z, h] * factors[a]
            for d in range(2):
                if h in rs_heads(d, half - 1):
                    value = value + rrecv[a, d, half - 1, h].astype(F32)
            out[:, cols[h]] = value.astype(BF16)

    rs_step(0, 0)
    rs_v = 1
    deltas = u_send[...]
    for d in range(1, X):
        arrive(u_recv, es, er, d)
        deltas = deltas + u_recv[x_src[d]]
    delta = [deltas[h : h + 1] for h in range(2)]
    dqacc[...] = jnp.zeros_like(dqacc)

    def loop_grads(b, _):
        for h in range(2):
            g = (p_s[h, b] * (dp_s[h, b] - delta[h])).astype(BF16)
            queries = qbuf[:, :, cols[h]].reshape(Q, HDIM)
            kpart[b, h] = jnp.dot(g, queries, preferred_element_type=F32)
            dqacc[h] += jnp.dot(kt[b, cols[h], :], g, preferred_element_type=F32)
        return 0

    lax.fori_loop(0, Z, loop_grads, 0)
    rs_step(1, 0)
    for b in range(X):
        for h in range(2):
            part = dqacc[h, :, b * R : (b + 1) * R].T * scale
            acc[b, :, cols[h]] = part
            dqsend[b, :, cols[h]] = part.astype(BF16)
    exchange(lambda t: dqsend.at[t], dqrecv, gs, gr)
    for t in range(1, half):
        rs_step(0, t)
        rs_step(1, t)
    total = acc[x]
    for d in range(1, X):
        arrive(dqrecv, gs, gr, d)
        total = total + dqrecv[x_src[d]].astype(F32)
    dq_out[...] = total.astype(BF16)
    rs_end(0, dv_out)
    rs_end(1, dk_out)

    for copy in pending:
        copy.wait_send()
    for d, copy in relayed:

        @pl.when(d != 0)
        def _():
            copy().wait_send()


def body(X, Z, Y, queries, key_rows, value_rows, upstream, out_weight, group_ids):
    R, C = queries.shape
    U = upstream.shape[1]
    W = out_weight.shape[0]
    K2 = Y // X
    Q = X * R
    groups = group_ids.reshape(X * Z, R)
    vmem = pl.BlockSpec(memory_space=pltpu.VMEM)
    dma = pltpu.SemaphoreType.DMA
    V = pltpu.VMEM
    out = jax.ShapeDtypeStruct((R, C), BF16)
    scratch = [
        V((Y, R, U), BF16), V((K2, 2, X, R, U), BF16), V((Z, W, C), BF16), V((X, R, C), BF16),
        V((Z, R, C), BF16), V((Z, R, C), BF16), V((X, R, C), F32), V((X, R, C), BF16),
        V((X, R, C), BF16), V((X, R, C), BF16),
        V((8, Q), F32), V((X, 8, Q), F32), V((8, Q), F32), V((X, 8, Q), F32),
        V((Z, R, R), F32), V((Z, C, R), BF16), V((2, Z, R, Q), F32), V((2, Z, R, Q), F32),
        V((Z, 2, R, HDIM), F32), V((Z, 2, R, HDIM), F32),
        V((X, R, C), BF16), V((X, R, C), BF16), V((2, HDIM, Q), F32),
        V((2, 2, Z // 2, 2, R, HDIM), BF16), V((2, 2, Z // 2, 2, R, HDIM), BF16),
        dma((2, Y // 2, 2)), dma((2, Y // 2, 2)), dma((2, Z // 2, 2)), dma((2, Z // 2, 2)),
        dma((2, Z // 2, 2)), dma((2, Z // 2, 2)), dma((X,)), dma((X,)), dma((Y,)), dma((X, K2)),
        dma((K2,)), dma((K2,)),
        dma((X,)), dma((X,)), dma((X,)), dma((X,)), dma((X,)), dma((X,)), dma((X,)), dma((X,)),
        dma((X,)), dma((X,)), dma((2, 2, Z // 2)), dma((2, 2, Z // 2)),
    ]
    return pl.pallas_call(
        functools.partial(kernel, X, Z, Y),
        out_shape=(out, out, out),
        in_specs=[vmem] * 6,
        out_specs=(vmem, vmem, vmem),
        scratch_shapes=scratch,
        name="attention_backward",
        compiler_params=pltpu.CompilerParams(
            collective_id=0, has_side_effects=True, vmem_limit_bytes=48 * 2**20
        ),
    )(groups, queries, key_rows, value_rows, upstream, out_weight)


def solution(mesh):
    split = P("ctx", "head")
    X, Z, Y = 4, mesh.shape["ctx"] // 4, mesh.shape["head"] // 2
    return jax.shard_map(
        functools.partial(body, X, Z, Y),
        mesh=mesh,
        in_specs=(split, split, split, split, split, P()),
        out_specs=(split, split, split),
        check_vma=False,
    )
```

```python
import functools

import jax
import jax.numpy as jnp
from jax import lax
from jax.experimental import pallas as pl
from jax.experimental.pallas import tpu as pltpu
from jax.sharding import PartitionSpec as P

MESH = pl.DeviceIdType.MESH
HDIM = 128
LOG2E = 1.4426950408889634
MASKED = -1e30
FLOOR = -1e29
KV_STEPS = (2, 3)
NU, NW = 2, 2
F32 = jnp.float32
BF16 = jnp.bfloat16


def kernel(
    X, Z, Y,
    gid_in, q, k, v, up, w,
    dq_out, dk_out, dv_out,
    gid,
    ubuf, upx, wbuf, qbuf, kbuf, vbuf, acc, dsend, drecv, dobuf,
    ml_send, ml_recv, u_send, u_recv, kid, kt, p_s, dp_s, kpart, vpart,
    dqsend, dqrecv, dqacc, rsend, rrecv,
    us, ur, ws, wr, kvs, kvr, qs, qr, xs, xr, sbs, sbr,
    ds, dr_, os_, or_, ms, mr, es, er, gs, gr, rs, rr, ls,
):
    K2 = Y // X
    WB = X * Z // (2 * Y)
    R = q.shape[0]
    Q = X * R
    i, j = lax.axis_index("ctx"), lax.axis_index("head")
    x, z = lax.div(i, Z), lax.rem(i, Z)
    y, c = lax.div(j, 2), lax.rem(j, 2)

    def dev(xx, zz, yy, cc):
        return (xx * Z + zz, yy * 2 + cc)

    def add(a, b, n):
        return lax.rem(a + b + n, n)

    def remote(src, dst, s_sem, r_sem, device):
        return pltpu.make_async_remote_copy(
            src_ref=src, dst_ref=dst, send_sem=s_sem, recv_sem=r_sem,
            device_id=device, device_id_type=MESH,
        )

    z_dev = (dev(x, add(z, 1, Z), y, c), dev(x, add(z, -1, Z), y, c))
    y_dev = (dev(x, z, add(y, 1, Y), c), dev(x, z, add(y, -1, Y), c))
    x_dev = [None] + [dev(add(x, d, X), z, y, c) for d in range(1, X)]
    x_src = [add(x, -d, X) for d in range(X)]
    sibling = dev(x, z, y, 1 - c)

    loads = [
        pltpu.make_async_copy(src, dst, ls.at[n])
        for n, (src, dst) in enumerate([
            (up, ubuf.at[y]), (w, wbuf.at[z]), (k, kbuf.at[z]), (v, vbuf.at[z]),
            (q, qbuf.at[x]), (gid_in, gid),
        ])
    ]
    for load in loads:
        load.start()

    barrier = pltpu.get_barrier_semaphore()
    peers = [*z_dev, *y_dev, *x_dev[1:], sibling]
    for peer in peers:
        pl.semaphore_signal(barrier, inc=1, device_id=peer, device_id_type=MESH)
    pl.semaphore_wait(barrier, len(peers))
    for load in loads:
        load.wait()

    pending = []

    class Ring:
        def __init__(self, n, me, devs, nc, buf, s_sem, r_sem):
            self.n, self.me, self.devs = n, me, devs
            self.buf, self.s, self.r = buf, s_sem, r_sem
            self.last, self.nc = n // 2 - 1, nc

        def chunks(self, d, s):
            order = list(range(self.nc)) if d == 0 else list(range(self.nc))[::-1]
            return order[: self.nc // 2] if s == self.last else order

        def block(self, d, s):
            return add(self.me, -s if d == 0 else s, self.n)

        def send(self, d, s, h):
            b = self.block(d, s)
            copy = remote(
                self.buf(b, h), self.buf(b, h), self.s.at[d, s, h], self.r.at[d, s, h], self.devs[d]
            )
            copy.start()
            pending.append(copy)

        def begin(self, n):
            for d in range(2):
                if n < len(self.chunks(d, 0)):
                    self.send(d, 0, self.chunks(d, 0)[n])

        def step(self, s, n):
            for d in range(2):
                if n < len(self.chunks(d, s)):
                    h = self.chunks(d, s)[n]
                    b = self.block(d, s + 1)
                    remote(
                        self.buf(b, h), self.buf(b, h), self.s.at[d, s, h],
                        self.r.at[d, s, h], self.devs[d],
                    ).wait_recv()
                    if s < self.last and h in self.chunks(d, s + 1):
                        self.send(d, s + 1, h)

    uh, wh = up.shape[0] // NU, w.shape[0] // NW
    ring_u = Ring(
        Y, y, y_dev, NU,
        lambda b, h: ubuf.at[b, pl.ds(h * uh, uh)],
        us, ur,
    )
    ring_w = Ring(
        Z, z, z_dev, NW,
        lambda b, h: wbuf.at[b, pl.ds(h * wh, wh)],
        ws, wr,
    )
    ring_kv = Ring(
        Z, z, z_dev, 2,
        lambda b, h: (kbuf, vbuf)[h].at[b],
        kvs, kvr,
    )

    relayed = []

    def relay(block, src, n):
        xt, kk = lax.div(block, K2), lax.rem(block, K2)
        d = add(xt, -x, X)

        def copy():
            return remote(
                src, upx.at[kk, c, x], xs.at[n], xr.at[d, kk], dev(xt, z, y, c)
            )

        @pl.when(d != 0)
        def _():
            copy().start()

        @pl.when(d == 0)
        def _():
            pltpu.make_async_copy(src, upx.at[kk, c, x], xr.at[d, kk]).start()

        relayed.append((d, copy))

    def exchange(src, dst, s_sem, r_sem):
        for d in range(1, X):
            copy = remote(src(add(x, d, X)), dst.at[x], s_sem.at[d], r_sem.at[d], x_dev[d])
            copy.start()
            pending.append(copy)

    def arrive(dst, s_sem, r_sem, d):
        ref = dst.at[x_src[d]]
        remote(ref, ref, s_sem.at[d], r_sem.at[d], x_dev[d]).wait_recv()

    for n in range(max(NU, NW)):
        ring_u.begin(n)
        ring_w.begin(n)
    relay(y, ubuf.at[y], 0)
    exchange(lambda _: qbuf.at[x], qbuf, qs, qr)
    for s in range(max(Y, Z) // 2):
        for n in range(max(NU, NW)):
            if s < Y // 2:
                ring_u.step(s, n)
            if s < Z // 2:
                ring_w.step(s, n)
        if s == 0:
            for n in range(2):
                ring_kv.begin(n)
        if s < Y // 2:
            relay(ring_u.block(0, s + 1), ubuf.at[ring_u.block(0, s + 1)], 2 * s + 1)
            if s < Y // 2 - 1:
                relay(ring_u.block(1, s + 1), ubuf.at[ring_u.block(1, s + 1)], 2 * s + 2)
        if s in KV_STEPS:
            for n in range(2):
                ring_kv.step(KV_STEPS.index(s), n)

    for b in range(Z):
        row = gid[pl.ds(x * Z + b, 1), :].astype(F32)
        kid[b] = jnp.broadcast_to(row, (R, R)).T
    qid = jnp.concatenate([gid[pl.ds(b * Z + z, 1), :].astype(F32) for b in range(X)], axis=1)

    turn = lax.rem(y - K2 * x + Y * K2, Y)
    near = jnp.where((turn >= 1) & (turn <= Y // 2), 1, 0) if K2 > 1 else 0
    order = [near, 1 - near] if K2 == 2 else list(range(K2))

    def shared(n, kk):
        return remote(upx.at[kk, c], upx.at[kk, c], sbs.at[n], sbr.at[n], sibling)

    for n, kk in enumerate(order):
        for d in range(X):
            dst = upx.at[kk, c, x_src[d]]
            remote(dst, dst, xs.at[0], xr.at[d, kk], sibling).wait_recv()
        copy = shared(n, kk)
        copy.start()
        pending.append(copy)
    if len(KV_STEPS) < Z // 2:
        for n in range(2):
            ring_kv.step(len(KV_STEPS), n)
    for n, kk in enumerate(order):
        shared(n, kk).wait_recv()
        total = None
        for cc in range(2):
            rows = upx[kk, cc].reshape(Q, upx.shape[4])
            weights = wbuf[pl.ds((kk * 2 + cc) * WB, WB)].reshape(upx.shape[4], w.shape[1])
            part = jnp.dot(rows, weights, preferred_element_type=F32)
            total = part if total is None else total + part
        total = total.reshape(acc.shape)
        if n > 0:
            total = total + acc[...]
        if n < K2 - 1:
            acc[...] = total
        else:
            acc[...] = total
            dsend[...] = total.astype(BF16)
    exchange(lambda t: dsend.at[t], drecv, ds, dr_)
    for t in range(len(KV_STEPS) + 1, Z // 2):
        for n in range(2):
            ring_kv.step(t, n)
    for d in range(1, X):
        arrive(qbuf, qs, qr, d)

    NT = (((1,), (1,)), ((), ()))
    scale = HDIM ** (-0.5)
    cols = [slice(h * HDIM, (h + 1) * HDIM) for h in range(2)]

    def fold(block, op):
        return op(block.reshape(R // 8, 8, Q), axis=0)

    def loop_scores(b, maxima):
        allowed = jnp.tile(kid[b], (1, X)) <= qid
        out = []
        for h in range(2):
            queries = qbuf[:, :, cols[h]].reshape(Q, HDIM)
            s = lax.dot_general(kbuf[b, :, cols[h]], queries, NT, preferred_element_type=F32)
            s = jnp.where(allowed, s * (scale * LOG2E), MASKED)
            p_s[h, b] = s
            kt[b, cols[h], :] = kbuf[b, :, cols[h]].T
            out.append(jnp.maximum(maxima[h], fold(s, jnp.max)))
        return tuple(out)

    start = jnp.full((8, Q), FLOOR, F32)
    maxima = lax.fori_loop(0, Z, loop_scores, (start, start))
    m_own = [jnp.max(m, axis=0, keepdims=True) for m in maxima]

    def loop_exp(b, sums):
        out = []
        for h in range(2):
            e = jnp.exp2(p_s[h, b] - m_own[h])
            p_s[h, b] = e
            out.append(sums[h] + fold(e, jnp.sum))
        return tuple(out)

    zero = jnp.zeros((8, Q), F32)
    sums = lax.fori_loop(0, Z, loop_exp, (zero, zero))
    l_own = [jnp.sum(s, axis=0, keepdims=True) for s in sums]
    ml_send[...] = jnp.concatenate([*m_own, *l_own, jnp.zeros((4, Q), F32)], axis=0)
    exchange(lambda _: ml_send, ml_recv, ms, mr)
    total = acc[x]
    for d in range(1, X):
        arrive(drecv, ds, dr_, d)
        total = total + drecv[x_src[d]].astype(F32)
    dobuf[x] = total.astype(BF16)
    exchange(lambda _: dobuf.at[x], dobuf, os_, or_)
    stats = [ml_send[...]]
    for d in range(1, X):
        arrive(ml_recv, ms, mr, d)
        stats.append(ml_recv[x_src[d]])
    factor = []
    for h in range(2):
        m_all = functools.reduce(jnp.maximum, [s[h : h + 1] for s in stats])
        l_all = sum(s[2 + h : 3 + h] * jnp.exp2(s[h : h + 1] - m_all) for s in stats)
        factor.append(jnp.exp2(m_own[h] - m_all) / l_all)

    for d in range(1, X):
        arrive(dobuf, os_, or_, d)

    def loop_probs(b, sums):
        out = []
        for h in range(2):
            grads = dobuf[:, :, cols[h]].reshape(Q, HDIM)
            g = lax.dot_general(vbuf[b, :, cols[h]], grads, NT, preferred_element_type=F32)
            prob = p_s[h, b] * factor[h]
            p_s[h, b] = prob
            dp_s[h, b] = g
            vpart[b, h] = jnp.dot(prob.astype(BF16), grads, preferred_element_type=F32)
            out.append(sums[h] + fold(prob * g, jnp.sum))
        return tuple(out)

    sums = lax.fori_loop(0, Z, loop_probs, (zero, zero))
    u_own = [jnp.sum(s, axis=0, keepdims=True) for s in sums]
    u_send[...] = jnp.concatenate([*u_own, jnp.zeros((6, Q), F32)], axis=0)
    exchange(lambda _: u_send, u_recv, es, er)

    half = Z // 2
    parts = (vpart, kpart)
    factors = (1.0, scale)

    def rs_heads(d, t):
        return (d,) if t == 0 else (0, 1)

    def rs_copy(a, d, t):
        if t == 0:
            src, dst = rsend.at[a, d, t, d], rrecv.at[a, d, t, d]
        else:
            src, dst = rsend.at[a, d, t], rrecv.at[a, d, t]
        return remote(src, dst, rs.at[a, d, t], rr.at[a, d, t], z_dev[d])

    def rs_step(a, t):
        for d in range(2):
            target = add(z, (half - t) if d == 0 else (t - half), Z)
            if t > 0:
                rs_copy(a, d, t - 1).wait_recv()
            for h in rs_heads(d, t):
                value = parts[a][target, h] * factors[a]
                if t > 0 and h in rs_heads(d, t - 1):
                    value = value + rrecv[a, d, t - 1, h].astype(F32)
                rsend[a, d, t, h] = value.astype(BF16)
            copy = rs_copy(a, d, t)
            copy.start()
            pending.append(copy)

    def rs_end(a, out):
        for d in range(2):
            rs_copy(a, d, half - 1).wait_recv()
        for h in range(2):
            value = parts[a][z, h] * factors[a]
            for d in range(2):
                if h in rs_heads(d, half - 1):
                    value = value + rrecv[a, d, half - 1, h].astype(F32)
            out[:, cols[h]] = value.astype(BF16)

    rs_step(0, 0)
    rs_v = 1
    deltas = u_send[...]
    for d in range(1, X):
        arrive(u_recv, es, er, d)
        deltas = deltas + u_recv[x_src[d]]
    delta = [deltas[h : h + 1] for h in range(2)]
    dqacc[...] = jnp.zeros_like(dqacc)

    def loop_grads(b, _):
        for h in range(2):
            g = (p_s[h, b] * (dp_s[h, b] - delta[h])).astype(BF16)
            queries = qbuf[:, :, cols[h]].reshape(Q, HDIM)
            kpart[b, h] = jnp.dot(g, queries, preferred_element_type=F32)
            dqacc[h] += jnp.dot(kt[b, cols[h], :], g, preferred_element_type=F32)
        return 0

    lax.fori_loop(0, Z, loop_grads, 0)
    rs_step(1, 0)
    for b in range(X):
        for h in range(2):
            part = dqacc[h, :, b * R : (b + 1) * R].T * scale
            acc[b, :, cols[h]] = part
            dqsend[b, :, cols[h]] = part.astype(BF16)
    exchange(lambda t: dqsend.at[t], dqrecv, gs, gr)
    for t in range(1, half):
        rs_step(0, t)
        rs_step(1, t)
    total = acc[x]
    for d in range(1, X):
        arrive(dqrecv, gs, gr, d)
        total = total + dqrecv[x_src[d]].astype(F32)
    dq_out[...] = total.astype(BF16)
    rs_end(0, dv_out)
    rs_end(1, dk_out)

    for copy in pending:
        copy.wait_send()
    for d, copy in relayed:

        @pl.when(d != 0)
        def _():
            copy().wait_send()


def deliver(*refs):
    sems = refs[6]
    copies = [pltpu.make_async_copy(refs[n], refs[n + 3], sems.at[n]) for n in range(3)]
    for copy in copies:
        copy.start()
    for copy in copies:
        copy.wait()


def body(X, Z, Y, queries, key_rows, value_rows, upstream, out_weight, group_ids):
    R, C = queries.shape
    U = upstream.shape[1]
    W = out_weight.shape[0]
    K2 = Y // X
    Q = X * R
    groups = group_ids.reshape(X * Z, R)
    vm = pl.BlockSpec(memory_space=pltpu.VMEM)
    hbm = pl.BlockSpec(memory_space=pl.ANY)
    dma = pltpu.SemaphoreType.DMA
    V = pltpu.VMEM
    out = jax.ShapeDtypeStruct((R, C), BF16)
    scratch = [
        V((X * Z, R), jnp.int32),
        V((Y, R, U), BF16), V((K2, 2, X, R, U), BF16), V((Z, W, C), BF16), V((X, R, C), BF16),
        V((Z, R, C), BF16), V((Z, R, C), BF16), V((X, R, C), F32), V((X, R, C), BF16),
        V((X, R, C), BF16), V((X, R, C), BF16),
        V((8, Q), F32), V((X, 8, Q), F32), V((8, Q), F32), V((X, 8, Q), F32),
        V((Z, R, R), F32), V((Z, C, R), BF16), V((2, Z, R, Q), F32), V((2, Z, R, Q), F32),
        V((Z, 2, R, HDIM), F32), V((Z, 2, R, HDIM), F32),
        V((X, R, C), BF16), V((X, R, C), BF16), V((2, HDIM, Q), F32),
        V((2, 2, Z // 2, 2, R, HDIM), BF16), V((2, 2, Z // 2, 2, R, HDIM), BF16),
        dma((2, Y // 2, NU)), dma((2, Y // 2, NU)), dma((2, Z // 2, NW)), dma((2, Z // 2, NW)),
        dma((2, Z // 2, 2)), dma((2, Z // 2, 2)), dma((X,)), dma((X,)), dma((Y,)), dma((X, K2)),
        dma((K2,)), dma((K2,)),
        dma((X,)), dma((X,)), dma((X,)), dma((X,)), dma((X,)), dma((X,)), dma((X,)), dma((X,)),
        dma((X,)), dma((X,)), dma((2, 2, Z // 2)), dma((2, 2, Z // 2)), dma((6,)),
    ]
    grads = pl.pallas_call(
        functools.partial(kernel, X, Z, Y),
        out_shape=(out, out, out),
        in_specs=[hbm] * 6,
        out_specs=(vm, vm, vm),
        scratch_shapes=scratch,
        name="attention_backward",
        compiler_params=pltpu.CompilerParams(
            collective_id=0, has_side_effects=True, vmem_limit_bytes=48*2**20
        ),
    )(*[pltpu.with_memory_space_constraint(a, pltpu.HBM) for a in (groups, queries, key_rows, value_rows, upstream, out_weight)])
    return pl.pallas_call(
        deliver,
        out_shape=(out, out, out),
        in_specs=[vm] * 3,
        out_specs=(hbm, hbm, hbm),
        scratch_shapes=[dma((3,))],
        name="deliver",
        compiler_params=pltpu.CompilerParams(vmem_limit_bytes=32*2**20),
    )(*grads)


def solution(mesh):
    split = P("ctx", "head")
    X, Z, Y = 4, mesh.shape["ctx"] // 4, mesh.shape["head"] // 2
    return jax.shard_map(
        functools.partial(body, X, Z, Y),
        mesh=mesh,
        in_specs=(split, split, split, split, split, P()),
        out_specs=(split, split, split),
        check_vma=False,
    )
```

```python
import functools

import jax
import jax.numpy as jnp
from jax import lax
from jax.experimental import pallas as pl
from jax.experimental.pallas import tpu as pltpu
from jax.sharding import PartitionSpec as P

MESH = pl.DeviceIdType.MESH
HDIM = 128
LOG2E = 1.4426950408889634
MASKED = -1e30
FLOOR = -1e29
FIRST = ("w0", "k0", "w1", "k1", "w2", "k2", "w3")
SECOND = (("k3",), ())
THIRD = ()
AHEAD = 1
UNROLL = 8
NW = 2
FAR = (0, 1, 7, 2, 6, 3, 5, 4)
F32 = jnp.float32
BF16 = jnp.bfloat16


def kernel(
    X, Z, Y,
    gid_in, q, k, v, up, w,
    dq_out, dk_out, dv_out,
    gid,
    ubuf, upx, wbuf, qbuf, kbuf, vbuf, acc, dsend, drecv, dobuf,
    ml_send, ml_recv, u_send, u_recv, kid, kt, p_s, dp_s, kpart, vpart,
    dqsend, dqrecv, rsend, rrecv,
    ws, wr, kvs, kvr, qs, qr, xs, xr, sbs, sbr,
    ds, dr_, os_, or_, ms, mr, es, er, gs, gr, rs, rr, ls,
):
    K2 = Y // X
    WB = X * Z // (2 * Y)
    R = q.shape[0]
    Q = X * R
    i, j = lax.axis_index("ctx"), lax.axis_index("head")
    x, z = lax.div(i, Z), lax.rem(i, Z)
    y, c = lax.div(j, 2), lax.rem(j, 2)

    def dev(xx, zz, yy, cc):
        return (xx * Z + zz, yy * 2 + cc)

    def add(a, b, n):
        return lax.rem(a + b + n, n)

    def remote(src, dst, s_sem, r_sem, device):
        return pltpu.make_async_remote_copy(
            src_ref=src, dst_ref=dst, send_sem=s_sem, recv_sem=r_sem,
            device_id=device, device_id_type=MESH,
        )

    z_dev = (dev(x, add(z, 1, Z), y, c), dev(x, add(z, -1, Z), y, c))
    xt, yk = lax.div(y, K2), lax.rem(y, K2)
    away = add(xt, -x, X)
    x_dev = [None] + [dev(add(x, d, X), z, y, c) for d in range(1, X)]
    x_src = [add(x, -d, X) for d in range(X)]
    sibling = dev(x, z, y, 1 - c)

    loads = [
        pltpu.make_async_copy(src, dst, ls.at[n])
        for n, (src, dst) in enumerate([
            (up, ubuf), (w, wbuf.at[z]), (k, kbuf.at[z]), (v, vbuf.at[z]),
            (q, qbuf.at[x]), (gid_in, gid),
        ])
    ]
    for load in loads:
        load.start()

    barrier = pltpu.get_barrier_semaphore()
    peers = [*z_dev, *x_dev[1:], sibling]
    for peer in peers:
        pl.semaphore_signal(barrier, inc=1, device_id=peer, device_id_type=MESH)
    for d in range(X):
        for kk in range(K2):

            @pl.when((d != 0) | (yk != kk) | (away != 0))
            def _():
                source = dev(add(x, d, X), z, K2 * x + kk, c)
                pl.semaphore_signal(barrier, inc=1, device_id=source, device_id_type=MESH)

    pl.semaphore_wait(barrier, len(peers) + X * K2 - jnp.where(away == 0, 1, 0))
    for load in loads:
        load.wait()

    pending = []

    class Ring:
        def __init__(self, n, me, devs, nc, buf, s_sem, r_sem):
            self.n, self.me, self.devs = n, me, devs
            self.buf, self.s, self.r = buf, s_sem, r_sem
            self.last, self.nc = n // 2 - 1, nc

        def chunks(self, d, s):
            order = list(range(self.nc)) if d == 0 else list(range(self.nc))[::-1]
            return order[: self.nc // 2] if s == self.last else order

        def block(self, d, s):
            return add(self.me, -s if d == 0 else s, self.n)

        def send(self, d, s, h):
            b = self.block(d, s)
            copy = remote(
                self.buf(b, h), self.buf(b, h), self.s.at[d, s, h], self.r.at[d, s, h], self.devs[d]
            )
            copy.start()
            pending.append(copy)

        def begin(self, n):
            for d in range(2):
                if n < len(self.chunks(d, 0)):
                    self.send(d, 0, self.chunks(d, 0)[n])

        def step(self, s, n):
            for d in range(2):
                if n < len(self.chunks(d, s)):
                    h = self.chunks(d, s)[n]
                    b = self.block(d, s + 1)
                    remote(
                        self.buf(b, h), self.buf(b, h), self.s.at[d, s, h],
                        self.r.at[d, s, h], self.devs[d],
                    ).wait_recv()
                    if s < self.last and h in self.chunks(d, s + 1):
                        self.send(d, s + 1, h)

    wh = w.shape[0] // NW
    ring_w = Ring(
        Z, z, z_dev, NW,
        lambda b, h: wbuf.at[b, pl.ds(h * wh, wh)],
        ws, wr,
    )
    ring_kv = Ring(
        Z, z, z_dev, 2,
        lambda b, h: (kbuf, vbuf)[h].at[b],
        kvs, kvr,
    )

    scattered = []

    def scatter(step):
        place = upx.at[yk, c, x]
        arrived = xr.at[away, yk]

        def copy():
            return remote(ubuf, place, xs.at[step], arrived, dev(xt, z, add(y, step, Y), c))

        if step > 0:
            copy().start()
            pending.append(copy())
        else:

            @pl.when(away != 0)
            def _():
                copy().start()

            @pl.when(away == 0)
            def _():
                pltpu.make_async_copy(ubuf, place, arrived).start()

            scattered.append((away, copy))

    def exchange(src, dst, s_sem, r_sem, pre=()):
        for d in range(1, X):
            copy = remote(
                src(add(x, d, X)), dst.at[(*pre, x)], s_sem.at[(*pre, d)], r_sem.at[(*pre, d)], x_dev[d]
            )
            copy.start()
            pending.append(copy)

    def arrive(dst, s_sem, r_sem, d, pre=()):
        ref = dst.at[(*pre, x_src[d])]
        remote(ref, ref, s_sem.at[(*pre, d)], r_sem.at[(*pre, d)], x_dev[d]).wait_recv()

    for step in FAR:
        scatter(step)
    for n in range(NW):
        ring_w.begin(n)
    for n in range(2):
        ring_kv.begin(n)
    exchange(lambda _: qbuf.at[x], qbuf, qs, qr)

    def run(steps):
        for step in steps:
            kind, s = step[0], int(step[1])
            if kind == "w" and s < Z // 2:
                for n in range(NW):
                    ring_w.step(s, n)
            if kind == "k" and s < Z // 2:
                for n in range(2):
                    ring_kv.step(s, n)

    run(FIRST)

    for b in range(Z):
        row = gid[pl.ds(x * Z + b, 1), :].astype(F32)
        kid[b] = jnp.broadcast_to(row, (R, R)).T
    qid = jnp.concatenate([gid[pl.ds(b * Z + z, 1), :].astype(F32) for b in range(X)], axis=1)

    turn = lax.rem(y - K2 * x + Y * K2, Y)
    near = jnp.where((turn >= 1) & (turn <= Y // 2), 1, 0) if K2 > 1 else 0
    order = [near, 1 - near] if K2 == 2 else list(range(K2))

    def shared(n, kk, d):
        piece = upx.at[kk, c, x_src[d]]
        return remote(piece, piece, sbs.at[n, d], sbr.at[n, d], sibling)

    turns = sorted(range(X), key=lambda d: min(d, X - d))
    for n, kk in enumerate(order):
        for d in turns:
            dst = upx.at[kk, c, x_src[d]]
            remote(dst, dst, xs.at[0], xr.at[d, kk], sibling).wait_recv()
            copy = shared(n, kk, d)
            copy.start()
            pending.append(copy)
        run(SECOND[n])
    cols = [slice(h * HDIM, (h + 1) * HDIM) for h in range(2)]
    for n, kk in enumerate(order):
        for d in turns:
            piece = upx.at[kk, 1 - c, x_src[d]]
            remote(piece, piece, sbs.at[n, d], sbr.at[n, d], sibling).wait_recv()
        total = None
        for cc in range(2):
            rows = upx[kk, cc].reshape(Q, upx.shape[4])
            weights = wbuf[pl.ds((kk * 2 + cc) * WB, WB)].reshape(upx.shape[4], w.shape[1])
            part = jnp.dot(rows, weights, preferred_element_type=F32)
            total = part if total is None else total + part
        total = total.reshape(X, R, 2 * HDIM)
        for h in range(2):
            value = total[:, :, cols[h]]
            if n > 0:
                value = value + acc[h]
            acc[h] = value
            if n == K2 - 1:
                dsend[h] = value.astype(BF16)
    for h in range(2):
        exchange(lambda t: dsend.at[h, t], drecv, ds, dr_, (h,))
    run(THIRD)
    for d in range(1, X):
        arrive(qbuf, qs, qr, d)

    NT = (((1,), (1,)), ((), ()))
    scale = HDIM ** (-0.5)

    def fold(block, op):
        return op(block.reshape(R // 8, 8, Q), axis=0)

    def loop_scores(b, maxima):
        allowed = jnp.tile(kid[b], (1, X)) <= qid
        out = []
        for h in range(2):
            queries = qbuf[:, :, cols[h]].reshape(Q, HDIM)
            s = lax.dot_general(kbuf[b, :, cols[h]], queries, NT, preferred_element_type=F32)
            s = jnp.where(allowed, s * (scale * LOG2E), MASKED)
            p_s[h, b] = s
            kt[b, cols[h], :] = kbuf[b, :, cols[h]].T
            out.append(jnp.maximum(maxima[h], fold(s, jnp.max)))
        return tuple(out)

    start = jnp.full((8, Q), FLOOR, F32)
    maxima = lax.fori_loop(0, Z, loop_scores, (start, start), unroll=UNROLL)
    m_own = [jnp.max(m, axis=0, keepdims=True) for m in maxima]

    def loop_exp(b, sums):
        out = []
        for h in range(2):
            e = jnp.exp2(p_s[h, b] - m_own[h])
            p_s[h, b] = e
            out.append(sums[h] + fold(e, jnp.sum))
        return tuple(out)

    zero = jnp.zeros((8, Q), F32)
    sums = lax.fori_loop(0, Z, loop_exp, (zero, zero), unroll=UNROLL)
    l_own = [jnp.sum(s, axis=0, keepdims=True) for s in sums]
    ml_send[...] = jnp.concatenate([*m_own, *l_own, jnp.zeros((4, Q), F32)], axis=0)
    exchange(lambda _: ml_send, ml_recv, ms, mr)
    for h in range(2):
        total = acc[h, x]
        for d in turns[1:]:
            arrive(drecv, ds, dr_, d, (h,))
            total = total + drecv[h, x_src[d]].astype(F32)
        dobuf[h, x] = total.astype(BF16)
        exchange(lambda _: dobuf.at[h, x], dobuf, os_, or_, (h,))
    stats = [ml_send[...]]
    for d in range(1, X):
        arrive(ml_recv, ms, mr, d)
        stats.append(ml_recv[x_src[d]])
    factor = []
    for h in range(2):
        m_all = functools.reduce(jnp.maximum, [s[h : h + 1] for s in stats])
        l_all = sum(s[2 + h : 3 + h] * jnp.exp2(s[h : h + 1] - m_all) for s in stats)
        factor.append(jnp.exp2(m_own[h] - m_all) / l_all)

    half = Z // 2
    parts = (vpart, kpart)
    factors = (1.0, scale)

    def rs_first(d, h):
        return 0 if h == d else 1

    def rs_copy(a, d, t, h):
        at = (a, d, t, h)
        return remote(rsend.at[at], rrecv.at[at], rs.at[at], rr.at[at], z_dev[d])

    def rs_step(a, d, h, stage):
        t = rs_first(d, h) + stage
        if t >= half:
            return
        target = add(z, (half - t) if d == 0 else (t - half), Z)
        value = parts[a][target, h] * factors[a]
        if stage > 0:
            rs_copy(a, d, t - 1, h).wait_recv()
            value = value + rrecv[a, d, t - 1, h].astype(F32)
        rsend[a, d, t, h] = value.astype(BF16)
        copy = rs_copy(a, d, t, h)
        copy.start()
        pending.append(copy)

    def rs_end(a, out):
        for h in range(2):
            value = parts[a][z, h] * factors[a]
            for d in range(2):
                if rs_first(d, h) < half:
                    rs_copy(a, d, half - 1, h).wait_recv()
                    value = value + rrecv[a, d, half - 1, h].astype(F32)
            out[:, cols[h]] = value.astype(BF16)

    def rs_stage(a, stage):
        for n in range(2):
            for d in range(2):
                rs_step(a, d, (d, 1 - d)[n], stage)

    for h in range(2):
        for d in turns[1:]:
            arrive(dobuf, os_, or_, d, (h,))

        def loop_probs(b, total):
            grads = dobuf[h].reshape(Q, HDIM)
            g = lax.dot_general(vbuf[b, :, cols[h]], grads, NT, preferred_element_type=F32)
            prob = p_s[h, b] * factor[h]
            p_s[h, b] = prob
            dp_s[h, b] = g
            vpart[b, h] = jnp.dot(prob.astype(BF16), grads, preferred_element_type=F32)
            return total + fold(prob * g, jnp.sum)

        total = lax.fori_loop(0, Z, loop_probs, zero, unroll=UNROLL)
        u_send[h] = total
        exchange(lambda _: u_send.at[h], u_recv, es, er, (h,))
        for d in range(2):
            rs_step(0, d, h, 0)
    for stage in range(1, AHEAD):
        rs_stage(0, stage)

    for h in range(2):
        total = u_send[h]
        for d in turns[1:]:
            arrive(u_recv, es, er, d, (h,))
            total = total + u_recv[h, x_src[d]]
        delta = jnp.sum(total, axis=0, keepdims=True)

        def loop_grads(b, total):
            g = (p_s[h, b] * (dp_s[h, b] - delta)).astype(BF16)
            queries = qbuf[:, :, cols[h]].reshape(Q, HDIM)
            kpart[b, h] = jnp.dot(g, queries, preferred_element_type=F32)
            return total + jnp.dot(kt[b, cols[h], :], g, preferred_element_type=F32)

        dq = lax.fori_loop(0, Z, loop_grads, jnp.zeros((HDIM, Q), F32), unroll=UNROLL)
        for d in range(2):
            rs_step(1, d, h, 0)
        for b in range(X):
            part = dq[:, b * R : (b + 1) * R].T * scale
            acc[h, b] = part
            dqsend[h, b] = part.astype(BF16)
        exchange(lambda t: dqsend.at[h, t], dqrecv, gs, gr, (h,))
    for stage in range(1, half):
        if stage + AHEAD - 1 < half:
            rs_stage(0, stage + AHEAD - 1)
        rs_stage(1, stage)
    for h in range(2):
        total = acc[h, x]
        for d in turns[1:]:
            arrive(dqrecv, gs, gr, d, (h,))
            total = total + dqrecv[h, x_src[d]].astype(F32)
        dq_out[:, cols[h]] = total.astype(BF16)
    rs_end(0, dv_out)
    rs_end(1, dk_out)

    for copy in pending:
        copy.wait_send()
    for d, copy in scattered:

        @pl.when(d != 0)
        def _():
            copy().wait_send()


def deliver(*refs):
    sems = refs[6]
    copies = [pltpu.make_async_copy(refs[n], refs[n + 3], sems.at[n]) for n in range(3)]
    for copy in copies:
        copy.start()
    for copy in copies:
        copy.wait()


def body(X, Z, Y, queries, key_rows, value_rows, upstream, out_weight, group_ids):
    R, C = queries.shape
    U = upstream.shape[1]
    W = out_weight.shape[0]
    K2 = Y // X
    Q = X * R
    groups = group_ids.reshape(X * Z, R)
    vm = pl.BlockSpec(memory_space=pltpu.VMEM)
    hbm = pl.BlockSpec(memory_space=pl.ANY)
    dma = pltpu.SemaphoreType.DMA
    V = pltpu.VMEM
    out = jax.ShapeDtypeStruct((R, C), BF16)
    scratch = [
        V((X * Z, R), jnp.int32),
        V((R, U), BF16), V((K2, 2, X, R, U), BF16), V((Z, W, C), BF16), V((X, R, C), BF16),
        V((Z, R, C), BF16), V((Z, R, C), BF16), V((2, X, R, HDIM), F32), V((2, X, R, HDIM), BF16),
        V((2, X, R, HDIM), BF16), V((2, X, R, HDIM), BF16),
        V((8, Q), F32), V((X, 8, Q), F32), V((2, 8, Q), F32), V((2, X, 8, Q), F32),
        V((Z, R, R), F32), V((Z, C, R), BF16), V((2, Z, R, Q), F32), V((2, Z, R, Q), F32),
        V((Z, 2, R, HDIM), F32), V((Z, 2, R, HDIM), F32),
        V((2, X, R, HDIM), BF16), V((2, X, R, HDIM), BF16),
        V((2, 2, Z // 2, 2, R, HDIM), BF16), V((2, 2, Z // 2, 2, R, HDIM), BF16),
        dma((2, Z // 2, NW)), dma((2, Z // 2, NW)),
        dma((2, Z // 2, 2)), dma((2, Z // 2, 2)), dma((X,)), dma((X,)), dma((Y,)), dma((X, K2)),
        dma((K2, X)), dma((K2, X)),
        dma((2, X)), dma((2, X)), dma((2, X)), dma((2, X)), dma((X,)), dma((X,)), dma((2, X)), dma((2, X)),
        dma((2, X)), dma((2, X)), dma((2, 2, Z // 2, 2)), dma((2, 2, Z // 2, 2)), dma((6,)),
    ]
    grads = pl.pallas_call(
        functools.partial(kernel, X, Z, Y),
        out_shape=(out, out, out),
        in_specs=[hbm] * 6,
        out_specs=(vm, vm, vm),
        scratch_shapes=scratch,
        name="attention_backward",
        compiler_params=pltpu.CompilerParams(
            collective_id=0, has_side_effects=True, vmem_limit_bytes=48*2**20
        ),
    )(*[pltpu.with_memory_space_constraint(a, pltpu.HBM) for a in (groups, queries, key_rows, value_rows, upstream, out_weight)])
    return pl.pallas_call(
        deliver,
        out_shape=(out, out, out),
        in_specs=[vm] * 3,
        out_specs=(hbm, hbm, hbm),
        scratch_shapes=[dma((3,))],
        name="deliver",
        compiler_params=pltpu.CompilerParams(vmem_limit_bytes=32*2**20),
    )(*grads)


def solution(mesh):
    split = P("ctx", "head")
    X, Z, Y = 4, mesh.shape["ctx"] // 4, mesh.shape["head"] // 2
    return jax.shard_map(
        functools.partial(body, X, Z, Y),
        mesh=mesh,
        in_specs=(split, split, split, split, split, P()),
        out_specs=(split, split, split),
        check_vma=False,
    )
```

```python
import functools

import jax
import jax.numpy as jnp
from jax import lax
from jax.experimental import pallas as pl
from jax.experimental.pallas import tpu as pltpu
from jax.sharding import PartitionSpec as P

MESH = pl.DeviceIdType.MESH
HDIM = 128
LOG2E = 1.4426950408889634
MASKED = -1e30
FLOOR = -1e29
FIRST = ("w0", "k0", "w1", "k1", "w2", "k2", "w3")
SECOND = (("k3",), ())
THIRD = ()
AHEAD = 1
UNROLL = 8
NW = 2
FAR = (0, 1, 7, 2, 6, 3, 5, 4)
F32 = jnp.float32
BF16 = jnp.bfloat16


def kernel(
    X, Z, Y,
    gid_in, q, k, v, up, w,
    dq_out, dk_out, dv_out,
    gid,
    ubuf, upx, wbuf, qbuf, kbuf, vbuf, acc, dsend, drecv, dobuf,
    ml_send, ml_recv, u_send, u_recv, kid, kt, p_s, dp_s, kpart, vpart,
    dqsend, dqrecv, rsend, rrecv,
    ws, wr, kvs, kvr, qs, qr, xs, xr, sbs, sbr,
    ds, dr_, os_, or_, ms, mr, es, er, gs, gr, rs, rr, ls,
):
    K2 = Y // X
    WB = X * Z // (2 * Y)
    R = q.shape[0]
    Q = X * R
    i, j = lax.axis_index("ctx"), lax.axis_index("head")
    x, z = lax.div(i, Z), lax.rem(i, Z)
    y, c = lax.div(j, 2), lax.rem(j, 2)

    def dev(xx, zz, yy, cc):
        return (xx * Z + zz, yy * 2 + cc)

    def add(a, b, n):
        return lax.rem(a + b + n, n)

    def remote(src, dst, s_sem, r_sem, device):
        return pltpu.make_async_remote_copy(
            src_ref=src, dst_ref=dst, send_sem=s_sem, recv_sem=r_sem,
            device_id=device, device_id_type=MESH,
        )

    z_dev = (dev(x, add(z, 1, Z), y, c), dev(x, add(z, -1, Z), y, c))
    xt, yk = lax.div(y, K2), lax.rem(y, K2)
    away = add(xt, -x, X)
    x_dev = [None] + [dev(add(x, d, X), z, y, c) for d in range(1, X)]
    x_src = [add(x, -d, X) for d in range(X)]
    sibling = dev(x, z, y, 1 - c)

    loads = [
        pltpu.make_async_copy(src, dst, ls.at[n])
        for n, (src, dst) in enumerate([
            (up, ubuf), (w, wbuf.at[z]), (k, kbuf.at[z]), (v, vbuf.at[z]),
            (q, qbuf.at[x]), (gid_in, gid),
        ])
    ]
    for load in loads:
        load.start()

    barrier = pltpu.get_barrier_semaphore()
    peers = [*z_dev, *x_dev[1:], sibling]
    for peer in peers:
        pl.semaphore_signal(barrier, inc=1, device_id=peer, device_id_type=MESH)
    for d in range(X):
        for kk in range(K2):

            @pl.when((d != 0) | (yk != kk) | (away != 0))
            def _():
                source = dev(add(x, d, X), z, K2 * x + kk, c)
                pl.semaphore_signal(barrier, inc=1, device_id=source, device_id_type=MESH)

    pl.semaphore_wait(barrier, len(peers) + X * K2 - jnp.where(away == 0, 1, 0))
    for load in loads:
        load.wait()

    pending = []

    class Ring:
        def __init__(self, n, me, devs, nc, buf, s_sem, r_sem):
            self.n, self.me, self.devs = n, me, devs
            self.buf, self.s, self.r = buf, s_sem, r_sem
            self.last, self.nc = n // 2 - 1, nc

        def chunks(self, d, s):
            order = list(range(self.nc)) if d == 0 else list(range(self.nc))[::-1]
            return order[: self.nc // 2] if s == self.last else order

        def block(self, d, s):
            return add(self.me, -s if d == 0 else s, self.n)

        def send(self, d, s, h):
            b = self.block(d, s)
            copy = remote(
                self.buf(b, h), self.buf(b, h), self.s.at[d, s, h], self.r.at[d, s, h], self.devs[d]
            )
            copy.start()
            pending.append(copy)

        def begin(self, n):
            for d in range(2):
                if n < len(self.chunks(d, 0)):
                    self.send(d, 0, self.chunks(d, 0)[n])

        def step(self, s, n):
            for d in range(2):
                if n < len(self.chunks(d, s)):
                    h = self.chunks(d, s)[n]
                    b = self.block(d, s + 1)
                    remote(
                        self.buf(b, h), self.buf(b, h), self.s.at[d, s, h],
                        self.r.at[d, s, h], self.devs[d],
                    ).wait_recv()
                    if s < self.last and h in self.chunks(d, s + 1):
                        self.send(d, s + 1, h)

    wh = w.shape[0] // NW
    ring_w = Ring(
        Z, z, z_dev, NW,
        lambda b, h: wbuf.at[b, pl.ds(h * wh, wh)],
        ws, wr,
    )
    ring_kv = Ring(
        Z, z, z_dev, 2,
        lambda b, h: (kbuf, vbuf)[h].at[b],
        kvs, kvr,
    )

    scattered = []

    def scatter(step):
        place = upx.at[yk, c, x]
        arrived = xr.at[away, yk]

        def copy():
            return remote(ubuf, place, xs.at[step], arrived, dev(xt, z, add(y, step, Y), c))

        if step > 0:
            copy().start()
            pending.append(copy())
        else:

            @pl.when(away != 0)
            def _():
                copy().start()

            @pl.when(away == 0)
            def _():
                pltpu.make_async_copy(ubuf, place, arrived).start()

            scattered.append((away, copy))

    def exchange(src, dst, s_sem, r_sem, pre=()):
        for d in range(1, X):
            copy = remote(
                src(add(x, d, X)), dst.at[(*pre, x)], s_sem.at[(*pre, d)], r_sem.at[(*pre, d)], x_dev[d]
            )
            copy.start()
            pending.append(copy)

    def arrive(dst, s_sem, r_sem, d, pre=()):
        ref = dst.at[(*pre, x_src[d])]
        remote(ref, ref, s_sem.at[(*pre, d)], r_sem.at[(*pre, d)], x_dev[d]).wait_recv()

    for n in range(NW):
        ring_w.begin(n)
    for step in FAR:
        scatter(step)
    for n in range(2):
        ring_kv.begin(n)
    exchange(lambda _: qbuf.at[x], qbuf, qs, qr)

    def run(steps):
        for step in steps:
            kind, s = step[0], int(step[1])
            if kind == "w" and s < Z // 2:
                for n in range(NW):
                    ring_w.step(s, n)
            if kind == "k" and s < Z // 2:
                for n in range(2):
                    ring_kv.step(s, n)

    run(FIRST)

    for b in range(Z):
        row = gid[pl.ds(x * Z + b, 1), :].astype(F32)
        kid[b] = jnp.broadcast_to(row, (R, R)).T
    qid = jnp.concatenate([gid[pl.ds(b * Z + z, 1), :].astype(F32) for b in range(X)], axis=1)

    turn = lax.rem(y - K2 * x + Y * K2, Y)
    near = jnp.where((turn >= 1) & (turn <= Y // 2), 1, 0) if K2 > 1 else 0
    order = [near, 1 - near] if K2 == 2 else list(range(K2))

    def shared(n, kk, d):
        piece = upx.at[kk, c, x_src[d]]
        return remote(piece, piece, sbs.at[n, d], sbr.at[n, d], sibling)

    turns = sorted(range(X), key=lambda d: min(d, X - d))
    for n, kk in enumerate(order):
        for d in turns:
            dst = upx.at[kk, c, x_src[d]]
            remote(dst, dst, xs.at[0], xr.at[d, kk], sibling).wait_recv()
            copy = shared(n, kk, d)
            copy.start()
            pending.append(copy)
        run(SECOND[n])
    cols = [slice(h * HDIM, (h + 1) * HDIM) for h in range(2)]
    for n, kk in enumerate(order):
        for d in turns:
            piece = upx.at[kk, 1 - c, x_src[d]]
            remote(piece, piece, sbs.at[n, d], sbr.at[n, d], sibling).wait_recv()
        total = None
        for cc in range(2):
            rows = upx[kk, cc].reshape(Q, upx.shape[4])
            weights = wbuf[pl.ds((kk * 2 + cc) * WB, WB)].reshape(upx.shape[4], w.shape[1])
            part = jnp.dot(rows, weights, preferred_element_type=F32)
            total = part if total is None else total + part
        total = total.reshape(X, R, 2 * HDIM)
        for h in range(2):
            value = total[:, :, cols[h]]
            if n > 0:
                value = value + acc[h]
            acc[h] = value
            if n == K2 - 1:
                dsend[h] = value.astype(BF16)
    for h in range(2):
        exchange(lambda t: dsend.at[h, t], drecv, ds, dr_, (h,))
    run(THIRD)
    for d in range(1, X):
        arrive(qbuf, qs, qr, d)

    NT = (((1,), (1,)), ((), ()))
    scale = HDIM ** (-0.5)

    def fold(block, op):
        return op(block.reshape(R // 8, 8, Q), axis=0)

    def loop_scores(b, maxima):
        allowed = jnp.tile(kid[b], (1, X)) <= qid
        out = []
        for h in range(2):
            queries = qbuf[:, :, cols[h]].reshape(Q, HDIM)
            s = lax.dot_general(kbuf[b, :, cols[h]], queries, NT, preferred_element_type=F32)
            s = jnp.where(allowed, s * (scale * LOG2E), MASKED)
            p_s[h, b] = s
            kt[b, cols[h], :] = kbuf[b, :, cols[h]].T
            out.append(jnp.maximum(maxima[h], fold(s, jnp.max)))
        return tuple(out)

    start = jnp.full((8, Q), FLOOR, F32)
    maxima = lax.fori_loop(0, Z, loop_scores, (start, start), unroll=UNROLL)
    m_own = [jnp.max(m, axis=0, keepdims=True) for m in maxima]

    def loop_exp(b, sums):
        out = []
        for h in range(2):
            e = jnp.exp2(p_s[h, b] - m_own[h])
            p_s[h, b] = e
            out.append(sums[h] + fold(e, jnp.sum))
        return tuple(out)

    zero = jnp.zeros((8, Q), F32)
    sums = lax.fori_loop(0, Z, loop_exp, (zero, zero), unroll=UNROLL)
    l_own = [jnp.sum(s, axis=0, keepdims=True) for s in sums]
    ml_send[...] = jnp.concatenate([*m_own, *l_own, jnp.zeros((4, Q), F32)], axis=0)
    exchange(lambda _: ml_send, ml_recv, ms, mr)
    for h in range(2):
        total = acc[h, x]
        for d in turns[1:]:
            arrive(drecv, ds, dr_, d, (h,))
            total = total + drecv[h, x_src[d]].astype(F32)
        dobuf[h, x] = total.astype(BF16)
        exchange(lambda _: dobuf.at[h, x], dobuf, os_, or_, (h,))
    stats = [ml_send[...]]
    for d in range(1, X):
        arrive(ml_recv, ms, mr, d)
        stats.append(ml_recv[x_src[d]])
    factor = []
    for h in range(2):
        m_all = functools.reduce(jnp.maximum, [s[h : h + 1] for s in stats])
        l_all = sum(s[2 + h : 3 + h] * jnp.exp2(s[h : h + 1] - m_all) for s in stats)
        factor.append(jnp.exp2(m_own[h] - m_all) / l_all)

    half = Z // 2
    parts = (vpart, kpart)
    factors = (1.0, scale)

    def rs_first(d, h):
        return 0 if h == d else 1

    def rs_copy(a, d, t, h):
        at = (a, d, t, h)
        return remote(rsend.at[at], rrecv.at[at], rs.at[at], rr.at[at], z_dev[d])

    def rs_step(a, d, h, stage):
        t = rs_first(d, h) + stage
        if t >= half:
            return
        target = add(z, (half - t) if d == 0 else (t - half), Z)
        value = parts[a][target, h] * factors[a]
        if stage > 0:
            rs_copy(a, d, t - 1, h).wait_recv()
            value = value + rrecv[a, d, t - 1, h].astype(F32)
        rsend[a, d, t, h] = value.astype(BF16)
        copy = rs_copy(a, d, t, h)
        copy.start()
        pending.append(copy)

    def rs_end(a, out):
        for h in range(2):
            value = parts[a][z, h] * factors[a]
            for d in range(2):
                if rs_first(d, h) < half:
                    rs_copy(a, d, half - 1, h).wait_recv()
                    value = value + rrecv[a, d, half - 1, h].astype(F32)
            out[:, cols[h]] = value.astype(BF16)

    def rs_stage(a, stage):
        for n in range(2):
            for d in range(2):
                rs_step(a, d, (d, 1 - d)[n], stage)

    for h in range(2):
        for d in turns[1:]:
            arrive(dobuf, os_, or_, d, (h,))

        def loop_probs(b, total):
            grads = dobuf[h].reshape(Q, HDIM)
            g = lax.dot_general(vbuf[b, :, cols[h]], grads, NT, preferred_element_type=F32)
            prob = p_s[h, b] * factor[h]
            p_s[h, b] = prob
            dp_s[h, b] = g
            vpart[b, h] = jnp.dot(prob.astype(BF16), grads, preferred_element_type=F32)
            return total + fold(prob * g, jnp.sum)

        total = lax.fori_loop(0, Z, loop_probs, zero, unroll=UNROLL)
        u_send[h] = total
        exchange(lambda _: u_send.at[h], u_recv, es, er, (h,))
        for d in range(2):
            rs_step(0, d, h, 0)
    for stage in range(1, AHEAD):
        rs_stage(0, stage)

    for h in range(2):
        total = u_send[h]
        for d in turns[1:]:
            arrive(u_recv, es, er, d, (h,))
            total = total + u_recv[h, x_src[d]]
        delta = jnp.sum(total, axis=0, keepdims=True)

        def loop_grads(b, total):
            g = (p_s[h, b] * (dp_s[h, b] - delta)).astype(BF16)
            queries = qbuf[:, :, cols[h]].reshape(Q, HDIM)
            kpart[b, h] = jnp.dot(g, queries, preferred_element_type=F32)
            return total + jnp.dot(kt[b, cols[h], :], g, preferred_element_type=F32)

        dq = lax.fori_loop(0, Z, loop_grads, jnp.zeros((HDIM, Q), F32), unroll=UNROLL)
        for d in range(2):
            rs_step(1, d, h, 0)
        for b in range(X):
            part = dq[:, b * R : (b + 1) * R].T * scale
            acc[h, b] = part
            dqsend[h, b] = part.astype(BF16)
        exchange(lambda t: dqsend.at[h, t], dqrecv, gs, gr, (h,))
    for stage in range(1, half):
        if stage + AHEAD - 1 < half:
            rs_stage(0, stage + AHEAD - 1)
        rs_stage(1, stage)
    for h in range(2):
        total = acc[h, x]
        for d in turns[1:]:
            arrive(dqrecv, gs, gr, d, (h,))
            total = total + dqrecv[h, x_src[d]].astype(F32)
        dq_out[:, cols[h]] = total.astype(BF16)
    rs_end(0, dv_out)
    rs_end(1, dk_out)

    for copy in pending:
        copy.wait_send()
    for d, copy in scattered:

        @pl.when(d != 0)
        def _():
            copy().wait_send()


def deliver(*refs):
    sems = refs[6]
    copies = [pltpu.make_async_copy(refs[n], refs[n + 3], sems.at[n]) for n in range(3)]
    for copy in copies:
        copy.start()
    for copy in copies:
        copy.wait()


def body(X, Z, Y, queries, key_rows, value_rows, upstream, out_weight, group_ids):
    R, C = queries.shape
    U = upstream.shape[1]
    W = out_weight.shape[0]
    K2 = Y // X
    Q = X * R
    groups = group_ids.reshape(X * Z, R)
    vm = pl.BlockSpec(memory_space=pltpu.VMEM)
    hbm = pl.BlockSpec(memory_space=pl.ANY)
    dma = pltpu.SemaphoreType.DMA
    V = pltpu.VMEM
    out = jax.ShapeDtypeStruct((R, C), BF16)
    scratch = [
        V((X * Z, R), jnp.int32),
        V((R, U), BF16), V((K2, 2, X, R, U), BF16), V((Z, W, C), BF16), V((X, R, C), BF16),
        V((Z, R, C), BF16), V((Z, R, C), BF16), V((2, X, R, HDIM), F32), V((2, X, R, HDIM), BF16),
        V((2, X, R, HDIM), BF16), V((2, X, R, HDIM), BF16),
        V((8, Q), F32), V((X, 8, Q), F32), V((2, 8, Q), F32), V((2, X, 8, Q), F32),
        V((Z, R, R), F32), V((Z, C, R), BF16), V((2, Z, R, Q), F32), V((2, Z, R, Q), F32),
        V((Z, 2, R, HDIM), F32), V((Z, 2, R, HDIM), F32),
        V((2, X, R, HDIM), BF16), V((2, X, R, HDIM), BF16),
        V((2, 2, Z // 2, 2, R, HDIM), BF16), V((2, 2, Z // 2, 2, R, HDIM), BF16),
        dma((2, Z // 2, NW)), dma((2, Z // 2, NW)),
        dma((2, Z // 2, 2)), dma((2, Z // 2, 2)), dma((X,)), dma((X,)), dma((Y,)), dma((X, K2)),
        dma((K2, X)), dma((K2, X)),
        dma((2, X)), dma((2, X)), dma((2, X)), dma((2, X)), dma((X,)), dma((X,)), dma((2, X)), dma((2, X)),
        dma((2, X)), dma((2, X)), dma((2, 2, Z // 2, 2)), dma((2, 2, Z // 2, 2)), dma((6,)),
    ]
    grads = pl.pallas_call(
        functools.partial(kernel, X, Z, Y),
        out_shape=(out, out, out),
        in_specs=[hbm] * 6,
        out_specs=(vm, vm, vm),
        scratch_shapes=scratch,
        name="attention_backward",
        compiler_params=pltpu.CompilerParams(
            collective_id=0, has_side_effects=True, vmem_limit_bytes=48*2**20
        ),
    )(*[pltpu.with_memory_space_constraint(a, pltpu.HBM) for a in (groups, queries, key_rows, value_rows, upstream, out_weight)])
    return pl.pallas_call(
        deliver,
        out_shape=(out, out, out),
        in_specs=[vm] * 3,
        out_specs=(hbm, hbm, hbm),
        scratch_shapes=[dma((3,))],
        name="deliver",
        compiler_params=pltpu.CompilerParams(vmem_limit_bytes=32*2**20),
    )(*grads)


def solution(mesh):
    split = P("ctx", "head")
    X, Z, Y = 4, mesh.shape["ctx"] // 4, mesh.shape["head"] // 2
    return jax.shard_map(
        functools.partial(body, X, Z, Y),
        mesh=mesh,
        in_specs=(split, split, split, split, split, P()),
        out_specs=(split, split, split),
        check_vma=False,
    )
```
